512 devices in a mesh: cells: 128 (over x, z, core), comp: 4 (over y).
Axes of the slice: x: 4, y: 4, z: 16, core: 2. Of those that a mesh axis runs over, the one named last changes fastest.
Arguments:
- fine_moments: bfloat16 [288, 65536], P(None, 'cells'), may hold values from -6 to 6
- translations: bfloat16 [16, 288, 288], P('comp'), may hold values from -0.09375 to 0.09375
- shifts_up: bfloat16 [8, 288, 288], replicated, may hold values from -0.375 to 0.375
- fine_pairs: int32 [3, 16, 98304], P(None, 'comp', 'cells'), may hold values from 0 to 511, as said below
- coarse_pairs: int32 [3, 16, 98304], P(None, 'comp', 'cells'), may hold values from 0 to 127, as said below
- child_links: int32 [2, 65536], P(None, 'cells'), may hold values from 0 to 16383, as said below
Outputs:
- fine_locals: float32 [288, 65536], P('comp', 'cells')
- coarse_moments: bfloat16 [288, 16384], P(None, 'cells')
- coarse_locals: float32 [288, 16384], P('comp', 'cells')
The draws below stay inside these ranges and needn't reach their ends.
Inputs may be any that keep to these rules, and one draw needn't show every extreme that they name: `fine_pairs`: rows 0 and 1 are cell indices within their owners: row 0 within the cells of index g of cells, row 1 within those of index h, where g and h are given by the slot position as in the reference program; row 2 is 1 for a live slot and 0 for an empty one. For every pair of owners and every class at most 6 slots are live; some such block is full in every draw. `coarse_pairs`: as for fine_pairs, with coarse cells. `child_links`: row 0 is the parent coarse cell of each fine cell, never falling along the fine cells; every coarse cell has 1 to 8 children; the parents of one device's fine cells are that device's coarse cells, except that at most its last 4 fine cells may belong to the first coarse cell of the next device. Row 1 is the child's octant, 0 to 7, distinct among the children of one parent.
All inputs are finite; a program needn't handle non-finite values.
Results may differ from the reference program's by a relative error of at most 0.005.
Values may be sent and summed in bfloat16 or wider, within the bound.
No kernel may reach another device: no remote copies, remote signals or barrier semaphores. Data moves between devices by JAX's collectives and lax.ppermute only.
A program may use at most 128 MiB of HBM per device.

```python
import jax
import jax.numpy as jnp
from jax import lax

F = 288
FINE_DEV = 512
COARSE_DEV = 128
CAP = 6
OFFSETS = 16
FINE_CELLS = 65536
COARSE_CELLS = 16384
N_CELLS = 128


def random_pairs(key, cells_dev):
    subkeys = jax.random.split(key, 3)
    table_shape = (OFFSETS, N_CELLS * N_CELLS * CAP)
    position = jnp.arange(N_CELLS * N_CELLS * CAP, dtype=jnp.int32)[None, :]
    first_owner = position // (N_CELLS * CAP)
    second_owner = position // CAP % N_CELLS
    first_cells = jax.random.randint(subkeys[0], table_shape, 0, cells_dev)
    second_cells = jax.random.randint(subkeys[1], table_shape, 0, cells_dev)
    ticket = jax.random.randint(subkeys[2], table_shape, 0, 1000)
    live = (first_owner == second_owner) | (ticket < 500)
    return jnp.stack([first_cells, second_cells, live.astype(jnp.int32)]).astype(jnp.int32)


def draw_fine_pairs(key, part):
    key = jax.random.fold_in(key, 5)
    return random_pairs(key, FINE_DEV)


def draw_coarse_pairs(key, part):
    key = jax.random.fold_in(key, 7)
    return random_pairs(key, COARSE_DEV)


def draw_child_links(key, part):
    key = jax.random.fold_in(key, 11)
    subkeys = jax.random.split(key, 4)
    index_all = jnp.arange(N_CELLS + 1, dtype=jnp.int32)
    straddle = jax.random.randint(subkeys[0], (N_CELLS + 1,), 1, 5)
    forced = jax.random.randint(subkeys[1], (), 1, N_CELLS)
    straddle = jnp.where(index_all == forced, 4, straddle)
    straddle = jnp.where((index_all == 0) | (index_all == N_CELLS), 0, straddle)
    swing = jax.random.randint(subkeys[2], (N_CELLS, (COARSE_DEV - 2) // 2), -3, 4)
    middle = jnp.stack([4 + swing, 4 - swing], axis=-1).reshape(N_CELLS, COARSE_DEV - 2)
    first_count = (3 + straddle[:-1])[:, None]
    last_count = (5 - straddle[1:])[:, None]
    counts = jnp.concatenate([first_count, middle, last_count], axis=1).reshape(-1).astype(jnp.int32)
    starts = (jnp.cumsum(counts) - counts).astype(jnp.int32)
    marks = jnp.zeros((FINE_CELLS,), jnp.int32).at[starts].add(1)
    parent = (jnp.cumsum(marks) - 1).astype(jnp.int32)
    position = jnp.arange(FINE_CELLS, dtype=jnp.int32) - starts[parent]
    scores = jax.random.randint(subkeys[3], (COARSE_CELLS, 8), 0, 1 << 20) * 8 + jnp.arange(8, dtype=jnp.int32)[None, :]
    order_rank = jnp.argsort(jnp.argsort(-scores, axis=1), axis=1)
    chosen = (order_rank < counts[:, None]).astype(jnp.int32)
    running = jnp.cumsum(chosen, axis=1)
    octant = jnp.sum((running[parent] <= position[:, None]).astype(jnp.int32), axis=1)
    return jnp.stack([parent, octant]).astype(jnp.int32)


def steps_of(stream_key, extent, cuts, least, top_value):
    factor_of, own = 1.0, jax.random.fold_in(stream_key, 6)
    for axis_at, shards_of in cuts:
        steps = jnp.exp(jax.random.uniform(jax.random.fold_in(own, axis_at), (shards_of,), jnp.float32, least / len(cuts), top_value / len(cuts)))
        factor_of = factor_of * jnp.repeat(steps, extent[axis_at] // shards_of).reshape([-1 if axis == axis_at else 1 for axis in range(len(extent))])
    return factor_of


def scatter_about(rng, extent, scale, most, cuts=(), kind=jnp.bfloat16):
    gain = steps_of(rng, extent, cuts, -0.22, 0.18) if cuts else 1.0
    result = jax.random.normal(rng, extent, jnp.float32) * scale * gain
    return jnp.minimum(jnp.maximum(result, -most), most).astype(kind)


def setup_inputs(seed: int = 0) -> dict:
    keys = jax.random.split(jax.random.key(seed), 7)
    fine_moments = scatter_about(keys[0], (F, FINE_CELLS), 1.0, 6.0, ((1, 128),))
    translations = scatter_about(keys[1], (OFFSETS, F, F), (16 * F) ** -0.5, 0.09375, ((0, 4),))
    shifts_up = scatter_about(keys[2], (8, F, F), F ** -0.5, 0.375)
    fine_pairs = draw_fine_pairs(jax.random.fold_in(keys[6], 71), 0)
    coarse_pairs = draw_coarse_pairs(jax.random.fold_in(keys[6], 71), 0)
    child_links = draw_child_links(jax.random.fold_in(keys[6], 71), 0)
    return {"fine_moments": fine_moments, "translations": translations, "shifts_up": shifts_up, "fine_pairs": fine_pairs, "coarse_pairs": coarse_pairs, "child_links": child_links}


def level_reference(moments, translations, pair_list, cells_dev, level_scale):
    width = moments.shape[0]
    position = jnp.arange(N_CELLS * N_CELLS * CAP, dtype=jnp.int32)
    first_owner = position // (N_CELLS * CAP)
    second_owner = (position // CAP) % N_CELLS
    gathered = jnp.zeros((width, moments.shape[1]), jnp.float32)
    for offset in range(OFFSETS):
        first_cell = (first_owner * cells_dev + pair_list[0, offset]).astype(jnp.int32)
        second_cell = (second_owner * cells_dev + pair_list[1, offset]).astype(jnp.int32)
        weight_live = pair_list[2, offset].astype(jnp.float32)
        matrix = translations[offset].astype(jnp.float32)
        first_rows = jnp.take(moments, first_cell, axis=1).astype(jnp.float32)
        second_rows = jnp.take(moments, second_cell, axis=1).astype(jnp.float32)
        to_second = jnp.dot(matrix, first_rows, precision=lax.Precision.HIGHEST) * level_scale * weight_live
        to_first = jnp.dot(matrix.T, second_rows, precision=lax.Precision.HIGHEST) * level_scale * weight_live
        gathered = gathered.at[:, second_cell].add(to_second)
        gathered = gathered.at[:, first_cell].add(to_first)
    return gathered


def reference(fine_moments, translations, shifts_up, fine_pairs, coarse_pairs, child_links):
    fine_locals = level_reference(fine_moments, translations, fine_pairs, FINE_DEV, 1.0)
    width = fine_moments.shape[0]
    parent = child_links[0].astype(jnp.int32)
    octant = child_links[1].astype(jnp.int32)
    placed = jnp.zeros((width, 8 * COARSE_CELLS), jnp.float32)
    placed = placed.at[:, octant * COARSE_CELLS + parent].set(fine_moments.astype(jnp.float32))
    placed = placed.reshape(width, 8, COARSE_CELLS)
    summed = jnp.einsum('ofi,ioc->fc', shifts_up.astype(jnp.float32), placed, precision=lax.Precision.HIGHEST)
    coarse_moments = summed.astype(jnp.bfloat16)
    coarse_locals = level_reference(coarse_moments, translations, coarse_pairs, COARSE_DEV, 0.5)
    return (fine_locals, coarse_moments, coarse_locals)
```

```python
import functools

import jax
import jax.numpy as jnp
from jax import lax
from jax.experimental import pallas as pl
from jax.experimental.pallas import tpu as pltpu
from jax.sharding import Mesh
from jax.sharding import PartitionSpec as P

CAP = 6
CELLS = ("x", "zh", "zl", "core")
BF16 = jnp.bfloat16
F32 = jnp.float32


def upward_kernel(moments_ref, slot_ref, shifts_ref, out_ref):
    octants, width, _ = shifts_ref.shape
    coarse = out_ref.shape[1]
    spots = octants * coarse
    rows = lax.broadcasted_iota(jnp.int32, (spots, slot_ref.shape[1]), 0)
    hot = (rows == slot_ref[0:1, :]).astype(BF16)
    placed = lax.dot_general(
        moments_ref[...], hot, (((1,), (1,)), ((), ())), preferred_element_type=F32
    ).astype(BF16)
    total = jnp.zeros((width, coarse), F32)
    for octant in range(octants):
        part = placed[:, octant * coarse : (octant + 1) * coarse]
        total = total + jnp.dot(shifts_ref[octant], part, preferred_element_type=F32)
    out_ref[...] = total.astype(BF16)


def upward(moments, child_links, shifts_up):
    width, fine = moments.shape
    coarse = fine // 4
    group = lax.axis_index(CELLS)
    devices = lax.axis_size(CELLS)
    parent = child_links[0] - group * coarse
    octant = child_links[1]
    inside = parent < coarse
    slot = jnp.where(inside, octant * coarse + parent, -1)
    code = jnp.where(inside, -1, octant)[-4:].astype(F32)
    edge = jnp.concatenate([moments[:, -4:].T.astype(F32), code[:, None]], axis=1)
    edge = lax.ppermute(edge, CELLS, [(i, i + 1) for i in range(devices - 1)])
    edge_code = edge[:, width].astype(jnp.int32)
    edge_slot = jnp.where(edge_code >= 0, edge_code * coarse, -1)
    edge_moments = edge[:, :width].T.astype(BF16)
    pad = 124
    slots = jnp.concatenate([slot, edge_slot, jnp.full((pad,), -1, jnp.int32)])
    extended = jnp.concatenate([moments, edge_moments, jnp.zeros((width, pad), BF16)], axis=1)
    return pl.pallas_call(
        upward_kernel,
        out_shape=jax.ShapeDtypeStruct((width, coarse), BF16),
        compiler_params=pltpu.CompilerParams(vmem_limit_bytes=48 * 1024 * 1024),
        cost_estimate=pl.CostEstimate(flops=8 * 10**8, bytes_accessed=2 * 10**6, transcendentals=0),
        name="upward",
    )(extended, slots.reshape(1, -1), shifts_up)


def level_kernel(core_ref, own_ref, other_ref, src_ref, dst_ref, ops_ref, out_ref, xt_ref, s_ref, *, scale):
    step = pl.program_id(0)
    height, cells = own_ref.shape[1:]
    owners = dst_ref.shape[1]
    z = (step % 4) * 4 + step // 4
    core = core_ref[0]
    cell = lax.broadcasted_iota(jnp.int32, (cells, 128), 0)
    for block_ref, side in ((own_ref, core), (other_ref, 1 - core)):
        index = src_ref[0, side]
        hot = jnp.concatenate(
            [(cell == index[s : s + 1, :]).astype(BF16) for s in range(CAP)], axis=1
        )
        picked = jnp.dot(block_ref[0], hot, preferred_element_type=F32)
        for s in range(CAP):
            row = ((z * 2 + side) * CAP + s) * 128
            xt_ref[pl.ds(pl.multiple_of(row, 128), 128), 0:height] = picked[:, s * 128 : (s + 1) * 128].T

    @pl.when(step == pl.num_programs(0) - 1)
    def _():
        target = lax.broadcasted_iota(jnp.int32, (cells, owners), 0)

        def pair(p, carry):
            rows = dst_ref[pl.ds(pl.multiple_of(p * 8, 8), 8), :]
            for g in range(4):
                parts = []
                for j in (g, 4 + g):
                    terms = xt_ref[pl.ds(p * 8 + j, owners, stride=128), :]
                    terms = terms.T[0:height].astype(BF16)
                    hot = (target == rows[j : j + 1, :]).astype(BF16)
                    parts.append(
                        lax.dot_general(
                            terms, hot, (((1,), (1,)), ((), ())), preferred_element_type=F32
                        )
                    )
                start = pl.multiple_of(p * (2 * height), 2 * height)
                s_ref[g, pl.ds(start, 2 * height), :] = jnp.concatenate(parts, axis=0).astype(BF16)
            return carry

        lax.fori_loop(0, 16, pair, 0)
        for g in range(4):
            total = jnp.dot(ops_ref[...], s_ref[g], preferred_element_type=F32)
            out_ref[g] = (total * scale).astype(BF16)


def spread_along_z(block):
    def spread(array, axis):
        copies = jnp.broadcast_to(array[None], (4,) + array.shape)
        return lax.all_to_all(copies, axis, 0, 0, tiled=True)

    own = spread(spread(block, "zh"), "zl")
    own = own.reshape((16,) + block.shape)
    other = lax.ppermute(own, "core", [(0, 1), (1, 0)])
    return own, other


def level_partial(moments, src, dst, operators, scale):
    width, cells = moments.shape
    height = width // 4
    rows = lax.dynamic_slice_in_dim(moments, lax.axis_index("comp") * height, height, 0)
    own, other = spread_along_z(rows)
    core = lax.axis_index("core").reshape(1)
    owners = dst.shape[1]
    return pl.pallas_call(
        functools.partial(level_kernel, scale=scale),
        grid=(16,),
        in_specs=[
            pl.BlockSpec(memory_space=pltpu.SMEM),
            pl.BlockSpec((1, height, cells), lambda i: (i, 0, 0)),
            pl.BlockSpec((1, height, cells), lambda i: (i, 0, 0)),
            pl.BlockSpec((1, 2, 8, 128), lambda i: ((i % 4) * 4 + i // 4, 0, 0, 0)),
            pl.BlockSpec(dst.shape, lambda i: (0, 0)),
            pl.BlockSpec(operators.shape, lambda i: (0, 0)),
        ],
        out_specs=pl.BlockSpec((4, width, cells), lambda i: (0, 0, 0)),
        out_shape=jax.ShapeDtypeStruct((4, width, cells), BF16),
        scratch_shapes=[
            pltpu.VMEM((owners * 128, 128), F32),
            pltpu.VMEM((4, 32 * height, cells), BF16),
        ],
        compiler_params=pltpu.CompilerParams(vmem_limit_bytes=56 * 1024 * 1024),
        cost_estimate=pl.CostEstimate(flops=3 * 10**9, bytes_accessed=6 * 10**6, transcendentals=0),
        name="level",
    )(core, own, other, src, dst, operators)


def summed_over_parts(partial):
    groups, width, cells = partial.shape
    pieces = partial.reshape(groups * 4, width // 4, cells)
    pieces = lax.all_to_all(pieces, ("x", "comp"), 0, 0, tiled=True)
    return jnp.sum(pieces.astype(F32), axis=0)


def slot_lists(fine_pairs, coarse_pairs):
    both = jnp.stack([fine_pairs, coarse_pairs])
    first, second, alive = both[:, 0], both[:, 1], both[:, 2] == 1
    classes = first.shape[1]
    near = jnp.stack([jnp.where(alive, second, -1), first], axis=1)
    near = near.reshape(4 * classes, 4, 192).transpose(1, 0, 2)
    near = lax.all_to_all(near, "x", 0, 0, tiled=True)
    far = jnp.stack([jnp.where(alive, first, -1), second], axis=1)
    far = far.reshape(2, 2, classes, 4, 32, CAP).transpose(4, 0, 1, 2, 3, 5).reshape(32, 3, 128)
    far = lax.all_to_all(far, ("zh", "zl", "core"), 0, 0, tiled=True)
    gathered = lax.all_gather(
        jnp.concatenate([near.reshape(-1, 128), far.reshape(-1, 128)]), "comp"
    )
    near = gathered[:, :96].reshape(4, 4, 2, 2, classes, 192)
    far = gathered[:, 96:].reshape(4, 32, 2, 2, classes, 4, CAP)
    near_src = near[:, :, :, 0].transpose(2, 4, 0, 3, 1).reshape(2, 32, CAP, 64)
    near_dst = near[:, :, :, 1].transpose(2, 0, 3, 1, 4).reshape(2, 64, 192)
    far_src = far[:, :, :, 0].transpose(2, 1, 5, 0, 3, 4).reshape(2, 32, CAP, 64)
    far_dst = far[:, :, :, 1].transpose(2, 0, 3, 4, 1, 5).reshape(2, 64, 192)
    src = jnp.concatenate([near_src, far_src], axis=3)
    src = jnp.pad(src, ((0, 0), (0, 0), (0, 8 - CAP), (0, 0)), constant_values=-1)
    src = src.reshape(2, 16, 2, 8, 128)
    dst = jnp.concatenate([near_dst, far_dst], axis=1)
    return src, dst


def operator_columns(translations):
    width = translations.shape[1]
    height = width // 4
    every = lax.all_gather(translations, "comp", tiled=True)
    start = lax.axis_index("comp") * height
    to_first = lax.dynamic_slice_in_dim(every, start, height, 1).transpose(2, 0, 1)
    to_second = lax.dynamic_slice_in_dim(every, start, height, 2).transpose(1, 0, 2)
    return jnp.concatenate([to_first.reshape(width, -1), to_second.reshape(width, -1)], axis=1)


def per_device(fine_moments, translations, shifts_up, fine_pairs, coarse_pairs, child_links):
    src, dst = slot_lists(fine_pairs, coarse_pairs)
    operators = operator_columns(translations)
    coarse_moments = upward(fine_moments, child_links, shifts_up)
    fine_partial = level_partial(fine_moments, src[0], dst[0], operators, 1.0)
    coarse_partial = level_partial(coarse_moments, src[1], dst[1], operators, 0.5)
    return (summed_over_parts(fine_partial), coarse_moments, summed_over_parts(coarse_partial))


def solution(mesh):
    split = Mesh(mesh.devices.reshape(4, 4, 4, 2, 4), CELLS + ("comp",))
    return jax.shard_map(
        per_device,
        mesh=split,
        in_specs=(
            P(None, CELLS),
            P("comp", None, None),
            P(),
            P(None, "comp", CELLS),
            P(None, "comp", CELLS),
            P(None, CELLS),
        ),
        out_specs=(P("comp", CELLS), P(None, CELLS), P("comp", CELLS)),
        check_vma=False,
    )
```

```python
import functools

import jax
import jax.numpy as jnp
from jax import lax
from jax.experimental import pallas as pl
from jax.experimental.pallas import tpu as pltpu
from jax.sharding import Mesh
from jax.sharding import PartitionSpec as P

CAP = 6
CODE_OFFSET = 256
NO_CELL = 1024
CELLS = ("x", "zh", "zl", "core")
BF16 = jnp.bfloat16
F32 = jnp.float32


def upward_kernel(moments_ref, slot_ref, shifts_ref, out_ref):
    octants, width, _ = shifts_ref.shape
    coarse = out_ref.shape[1]
    spots = octants * coarse
    rows = lax.broadcasted_iota(jnp.int32, (spots, slot_ref.shape[1]), 0)
    hot = (rows == slot_ref[0:1, :]).astype(BF16)
    placed = lax.dot_general(
        moments_ref[...], hot, (((1,), (1,)), ((), ())), preferred_element_type=F32
    ).astype(BF16)
    total = jnp.zeros((width, coarse), F32)
    for octant in range(octants):
        part = placed[:, octant * coarse : (octant + 1) * coarse]
        total = total + jnp.dot(shifts_ref[octant], part, preferred_element_type=F32)
    out_ref[...] = total.astype(BF16)


def edge_from_before(moments, child_links):
    coarse = moments.shape[1] // 4
    group = lax.axis_index(CELLS)
    devices = lax.axis_size(CELLS)
    parent = child_links[0] - group * coarse
    octant = child_links[1]
    inside = parent < coarse
    slot = jnp.where(inside, octant * coarse + parent, -1)
    code = jnp.where(inside, -1, octant)[-4:].astype(F32)
    edge = jnp.concatenate([moments[:, -4:].T.astype(F32), code[:, None]], axis=1)
    return slot, lax.ppermute(edge, CELLS, [(i, i + 1) for i in range(devices - 1)])


def upward(moments, slot, edge, shifts_up):
    width, fine = moments.shape
    coarse = fine // 4
    edge_code = edge[:, width].astype(jnp.int32)
    edge_slot = jnp.where(edge_code >= 0, edge_code * coarse, -1)
    edge_moments = edge[:, :width].T.astype(BF16)
    pad = 124
    slots = jnp.concatenate([slot, edge_slot, jnp.full((pad,), -1, jnp.int32)])
    extended = jnp.concatenate([moments, edge_moments, jnp.zeros((width, pad), BF16)], axis=1)
    return pl.pallas_call(
        upward_kernel,
        out_shape=jax.ShapeDtypeStruct((width, coarse), BF16),
        compiler_params=pltpu.CompilerParams(vmem_limit_bytes=48 * 1024 * 1024),
        cost_estimate=pl.CostEstimate(flops=8 * 10**8, bytes_accessed=2 * 10**6, transcendentals=0),
        name="upward",
    )(extended, slots.reshape(1, -1), shifts_up)


def one_hot(row, cells):
    count = row.shape[1]
    part = min(cells, 256)
    place = lax.broadcasted_iota(jnp.int32, (part, count), 0).astype(F32).astype(BF16)
    ones, zeros = jnp.ones((part, count), BF16), jnp.zeros((part, count), BF16)
    tiles = []
    for first in range(0, cells, part):
        wanted = jnp.broadcast_to((row - first).astype(F32), (part, count)).astype(BF16)
        tiles.append(jnp.where(place == wanted, ones, zeros))
    return tiles[0] if len(tiles) == 1 else jnp.concatenate(tiles, axis=0)


def regrouped(arrays, lane_bits):
    arrays = [arrays[-j % 16] for j in range(16)]
    for b in range(4):
        arrays = [
            jnp.where(lane_bits[b], arrays[(j - (1 << b)) % 16], arrays[j]) for j in range(16)
        ]
    return arrays


def level_kernel(*refs, pieces, scale):
    place_ref, order_ref = refs[:2]
    blocks = refs[2 : 2 + 2 * pieces]
    src_ref, dst_ref, ops_ref, out_ref, picked_ref, group_ref, sums_ref = refs[2 + 2 * pieces :]
    height, cells = ops_ref.shape[0] // 32, blocks[0].shape[2]
    core, me = place_ref[0], place_ref[1]

    first = 0
    for own_ref, other_ref in zip(blocks[0::2], blocks[1::2]):

        def pick(i, carry, own_ref=own_ref, other_ref=other_ref, first=first):
            z = order_ref[first + i]
            for block_ref, side in ((own_ref, core), (other_ref, 1 - core)):
                h = z * 2 + side
                block = block_ref[i]
                held = block.shape[0]
                for part in range(4):
                    row = src_ref[pl.ds(h, 1), part * 256 : (part + 1) * 256]
                    picked = jnp.dot(block, one_hot(row, cells), preferred_element_type=F32)
                    picked = picked.astype(BF16)
                    picked_ref[h, 2 * part, 0:held] = picked[:, 0:128]
                    picked_ref[h, 2 * part + 1, 0:held] = picked[:, 128:256]
            return carry

        lax.fori_loop(0, own_ref.shape[0], pick, 0)
        first += own_ref.shape[0]

    lane = lax.broadcasted_iota(jnp.int32, (16, 128), 1) // 8
    lane_bits = [(lane >> b) & 1 == 1 for b in range(4)]
    padded = group_ref.shape[1]

    def add_up(q, carry):
        for half in range(2):
            for top in range(0, padded, 16):
                rows = slice(top, top + 16)
                arrays = [picked_ref[half * 16 + j, q, rows, :] for j in range(16)]
                for j, array in enumerate(regrouped(arrays, lane_bits)):
                    group_ref[j, rows, half * 128 : (half + 1) * 128] = array
        for half in range(2):
            lists = dst_ref[pl.ds(pl.multiple_of(q * 16 + half * 8, 8), 8), :]
            for target in range(2):
                for couple in range(2):
                    sums = []
                    for j in (target * 4 + couple * 2, target * 4 + couple * 2 + 1):
                        sums.append(
                            lax.dot_general(
                                group_ref[half * 8 + j, 0:height],
                                one_hot(lists[j : j + 1, :], cells),
                                (((1,), (1,)), ((), ())),
                                preferred_element_type=F32,
                            )
                        )
                    distance = (me + 4 - q % 4) % 4
                    start = (distance * 2 + q // 4) * 2 + couple
                    start = pl.multiple_of(start * (2 * height), 2 * height)
                    sums_ref[half * 2 + target, pl.ds(start, 2 * height), :] = jnp.concatenate(
                        sums, axis=0
                    ).astype(BF16)
        return carry

    lax.fori_loop(0, 8, add_up, 0)
    operators = ops_ref[...].T
    for target in range(4):
        total = jnp.dot(operators, sums_ref[target], preferred_element_type=F32)
        out_ref[target] = (total * scale).astype(BF16)


def own_rows(moments):
    height = moments.shape[0] // 4
    return lax.dynamic_slice_in_dim(moments, lax.axis_index("comp") * height, height, 0)


def other_core(array):
    return lax.ppermute(array, "core", [(0, 1), (1, 0)])


def spread_to(block, axis):
    copies = jnp.broadcast_to(block[None], (4,) + block.shape)
    return lax.all_to_all(copies, axis, 0, 0, tiled=True)


def spread_at_once(block):
    copies = jnp.broadcast_to(block[None], (16,) + block.shape)
    return lax.all_to_all(copies, ("zh", "zl"), 0, 0, tiled=True)


def level_partial(pieces, order, src, dst, operators, scale):
    blocks = [block for own, other in pieces for block in (own, other)]
    cells = blocks[0].shape[2]
    width = operators.shape[1]
    height = width // 4
    padded = -(-height // 16) * 16
    smem = pl.BlockSpec(memory_space=pltpu.SMEM)
    vmem = pl.BlockSpec(memory_space=pltpu.VMEM)
    return pl.pallas_call(
        functools.partial(level_kernel, pieces=len(pieces), scale=scale),
        in_specs=[smem, smem] + [vmem] * (len(blocks) + 3),
        out_specs=vmem,
        out_shape=jax.ShapeDtypeStruct((4, width, cells), BF16),
        scratch_shapes=[
            pltpu.VMEM((32, 8, padded, 128), BF16),
            pltpu.VMEM((16, padded, 256), BF16),
            pltpu.VMEM((4, 32 * height, cells), BF16),
        ],
        compiler_params=pltpu.CompilerParams(vmem_limit_bytes=48 * 1024 * 1024),
        cost_estimate=pl.CostEstimate(
            flops=5 * 10**7 * cells, bytes_accessed=6 * 10**6, transcendentals=0
        ),
        name="level",
    )(jnp.stack([lax.axis_index("core"), lax.axis_index("comp")]), order, *blocks, src, dst, operators)


def summed_over_parts(partial):
    groups, width, cells = partial.shape
    pieces = partial.reshape(groups * 4, width // 4, cells)
    pieces = lax.all_to_all(pieces, ("x", "comp"), 0, 0, tiled=True)
    return jnp.sum(pieces.astype(F32), axis=0)


def turned(rows):
    return pltpu.roll(rows, 0, 1, stride=8, stride_axis=0)


def crossed(rows, lane_bits):
    rows = jnp.concatenate([rows[0:1]] + [rows[j : j + 1] for j in range(15, 0, -1)], axis=0)
    for b in range(4):
        rows = jnp.where(lane_bits[b], pltpu.roll(rows, 1 << b, 0), rows)
    return rows


def lists_kernel(x_ref, near_ref, far_ref, *out_refs):
    lane = lax.broadcasted_iota(jnp.int32, (16, 128), 1) // 8
    lane_bits = [(lane >> b) & 1 == 1 for b in range(4)]

    def cells_of(codes):
        return codes.astype(F32).astype(jnp.int32) + CODE_OFFSET

    for part in range(4):
        for half in range(2):
            near_lists = [cells_of(near_ref[part, (x_ref[0] + 4 - g) % 4, half]) for g in range(4)]
            for level in range(2):
                src_ref, dst_ref = out_refs[2 * level : 2 * level + 2]
                lanes = slice(half * 128, (half + 1) * 128)
                hs = slice(half * 16, (half + 1) * 16)

                def near(value):
                    kind = (level * 2 + value) * 4
                    return jnp.concatenate(
                        [lists[kind : kind + 4] for lists in near_lists], axis=0
                    )

                def far(value):
                    return cells_of(far_ref[part, level * 2 + value, hs, :])

                src_ref[hs, part * 128 : (part + 1) * 128] = crossed(
                    turned(near(0)), lane_bits
                )
                dst_ref[part * 16 : (part + 1) * 16, lanes] = turned(near(1))
                src_ref[hs, (part + 4) * 128 : (part + 5) * 128] = turned(far(0))
                dst_ref[(part + 4) * 16 : (part + 5) * 16, lanes] = crossed(
                    turned(far(1)), lane_bits
                )


def slot_messages(fine_pairs, coarse_pairs):
    both = jnp.stack([fine_pairs, coarse_pairs])
    first, second, alive = both[:, 0], both[:, 1], both[:, 2] == 1
    classes = first.shape[1]

    def slots(source, target):
        lists = jnp.stack([jnp.where(alive, source - CODE_OFFSET, NO_CELL), target - CODE_OFFSET], 1)
        lists = lists.astype(BF16).reshape(2, 2, classes, 4, 32, CAP)
        return jnp.pad(lists, [(0, 0)] * 5 + [(0, 8 - CAP)], constant_values=NO_CELL)

    near = slots(second, first).reshape(2, 2, classes, 4, 2, 128)
    near = near.transpose(3, 4, 0, 1, 2, 5).reshape(4, 8 * classes, 128)
    far = slots(first, second).transpose(4, 0, 1, 3, 2, 5).reshape(4, 4, 8, 128)
    far = jnp.concatenate([far[:, j] for j in range(4)], axis=-1)
    return near, far


def passed(array, axis, distance):
    if distance == 0:
        return array
    count = lax.axis_size(axis)
    return lax.ppermute(array, axis, [(i, (i + distance) % count) for i in range(count)])


def parts_for(array, name, axis):
    me = lax.axis_index(name)
    return [
        lax.dynamic_index_in_dim(array, (me + distance) % 4, axis, keepdims=False)
        for distance in range(4)
    ]


def exchanged(parts, name):
    return jnp.stack([passed(part, name, distance) for distance, part in enumerate(parts)])


def lists_from_chip_and_comp(near, blocks):
    rows = blocks[:, 72:].reshape(4, 4, 2, 4, -1)
    rows = lax.dynamic_slice_in_dim(rows, lax.axis_index("zl") * 128, 128, 4)
    rows = rows.transpose(2, 0, 1, 3, 4).reshape(2, 64, 128)
    near = jnp.broadcast_to(near.reshape(1, 128, 128), (2, 128, 128))
    rows = jnp.concatenate([rows, near], axis=1)
    rows = jnp.broadcast_to(rows[:, None], (2, 4, 192, 128)).reshape(8, 192, 128)
    rows = lax.all_to_all(rows, ("core", "comp"), 0, 0, tiled=True).reshape(2, 4, 192, 128)
    near = lax.dynamic_index_in_dim(rows[:, :, 64:], lax.axis_index("core"), 0, keepdims=False)
    far = rows[:, :, :64].reshape(2, 4, 4, 4, 4, 128).transpose(1, 4, 3, 2, 0, 5)
    return near.reshape(4, 4, 2, 16, 128), far.reshape(4, 4, 32, 128)


def slot_lists(near, far):
    vmem = pl.BlockSpec(memory_space=pltpu.VMEM)
    return pl.pallas_call(
        lists_kernel,
        in_specs=[pl.BlockSpec(memory_space=pltpu.SMEM), vmem, vmem],
        out_specs=[vmem] * 4,
        out_shape=[
            jax.ShapeDtypeStruct((32, 1024), jnp.int32),
            jax.ShapeDtypeStruct((128, 256), jnp.int32),
        ]
        * 2,
        name="lists",
    )(lax.axis_index("x").reshape(1), near, far)


def operator_parts(translations):
    classes, width, _ = translations.shape
    both = jnp.stack([translations, translations.swapaxes(1, 2)])
    return parts_for(both.reshape(2, classes, 4, width // 4, width), "comp", 2)


def per_device(fine_moments, translations, shifts_up, fine_pairs, coarse_pairs, child_links):
    near, far = slot_messages(fine_pairs, coarse_pairs)
    rows = own_rows(fine_moments)
    copies = jnp.broadcast_to(rows[None], (4,) + rows.shape)
    four = lax.all_to_all(jnp.concatenate([copies, far], axis=1), "zh", 0, 0, tiled=True)
    slot, edge = edge_from_before(fine_moments, child_links)
    near, operators = parts_for(near, "x", 0), operator_parts(translations)
    four, edge, near, operators = lax.optimization_barrier((four, edge, near, operators))
    fine = spread_to(four, "zl").reshape((16,) + four.shape[1:])
    near = exchanged(near, "x")
    operators = exchanged(operators, "comp").reshape(-1, fine_moments.shape[0])
    coarse_moments = upward(fine_moments, slot, edge, shifts_up)
    near, operators, coarse_rows, fine = lax.optimization_barrier(
        (near, operators, own_rows(coarse_moments), fine)
    )
    fine_other = other_core(fine)
    fine_src, fine_dst, coarse_src, coarse_dst = slot_lists(*lists_from_chip_and_comp(near, fine))
    coarse_rows, fine_src = lax.optimization_barrier((coarse_rows, fine_src))
    place = jnp.arange(16, dtype=jnp.int32)
    order = place % 4 * 4 + place // 4
    fine_partial = level_partial([(fine, fine_other)], order, fine_src, fine_dst, operators, 1.0)

    coarse = spread_at_once(coarse_rows)
    coarse, fine_partial = lax.optimization_barrier((coarse, fine_partial))
    other = other_core(coarse)
    coarse_partial = level_partial(
        [(coarse, other)], place, coarse_src, coarse_dst, operators, 0.5
    )
    fine_locals = summed_over_parts(fine_partial)
    coarse_partial, fine_locals = lax.optimization_barrier((coarse_partial, fine_locals))
    return (fine_locals, coarse_moments, summed_over_parts(coarse_partial))


def solution(mesh):
    split = Mesh(mesh.devices.reshape(4, 4, 4, 2, 4), CELLS + ("comp",))
    return jax.shard_map(
        per_device,
        mesh=split,
        in_specs=(
            P(None, CELLS),
            P("comp", None, None),
            P(),
            P(None, "comp", CELLS),
            P(None, "comp", CELLS),
            P(None, CELLS),
        ),
        out_specs=(P("comp", CELLS), P(None, CELLS), P("comp", CELLS)),
        check_vma=False,
    )
```

```python
import functools

import jax
import jax.numpy as jnp
from jax import lax
from jax.experimental import pallas as pl
from jax.experimental.pallas import tpu as pltpu
from jax.sharding import Mesh
from jax.sharding import PartitionSpec as P

CAP = 6
CODE_OFFSET = 256
NO_CELL = 1024
CELLS = ("x", "zh", "zl", "core")
BF16 = jnp.bfloat16
F32 = jnp.float32


def upward_kernel(moments_ref, slot_ref, shifts_ref, out_ref):
    octants, width, _ = shifts_ref.shape
    coarse = out_ref.shape[1]
    spots = octants * coarse
    rows = lax.broadcasted_iota(jnp.int32, (spots, slot_ref.shape[1]), 0)
    hot = (rows == slot_ref[0:1, :]).astype(BF16)
    placed = lax.dot_general(
        moments_ref[...], hot, (((1,), (1,)), ((), ())), preferred_element_type=F32
    ).astype(BF16)
    total = jnp.zeros((width, coarse), F32)
    for octant in range(octants):
        part = placed[:, octant * coarse : (octant + 1) * coarse]
        total = total + jnp.dot(shifts_ref[octant], part, preferred_element_type=F32)
    out_ref[...] = total.astype(BF16)


def edge_from_before(moments, child_links):
    coarse = moments.shape[1] // 4
    group = lax.axis_index(CELLS)
    devices = lax.axis_size(CELLS)
    parent = child_links[0] - group * coarse
    octant = child_links[1]
    inside = parent < coarse
    slot = jnp.where(inside, octant * coarse + parent, -1)
    code = jnp.where(inside, -1, octant)[-4:].astype(F32)
    edge = jnp.concatenate([moments[:, -4:].T.astype(F32), code[:, None]], axis=1)
    return slot, lax.ppermute(edge, CELLS, [(i, i + 1) for i in range(devices - 1)])


def upward(moments, slot, edge, shifts_up):
    width, fine = moments.shape
    coarse = fine // 4
    edge_code = edge[:, width].astype(jnp.int32)
    edge_slot = jnp.where(edge_code >= 0, edge_code * coarse, -1)
    edge_moments = edge[:, :width].T.astype(BF16)
    pad = 124
    slots = jnp.concatenate([slot, edge_slot, jnp.full((pad,), -1, jnp.int32)])
    extended = jnp.concatenate([moments, edge_moments, jnp.zeros((width, pad), BF16)], axis=1)
    return pl.pallas_call(
        upward_kernel,
        out_shape=jax.ShapeDtypeStruct((width, coarse), BF16),
        compiler_params=pltpu.CompilerParams(vmem_limit_bytes=48 * 1024 * 1024),
        cost_estimate=pl.CostEstimate(flops=8 * 10**8, bytes_accessed=2 * 10**6, transcendentals=0),
        name="upward",
    )(extended, slots.reshape(1, -1), shifts_up)


def one_hot(row, cells):
    count = row.shape[1]
    part = min(cells, 256)
    place = lax.broadcasted_iota(jnp.int32, (part, count), 0).astype(F32).astype(BF16)
    ones, zeros = jnp.ones((part, count), BF16), jnp.zeros((part, count), BF16)
    tiles = []
    for first in range(0, cells, part):
        wanted = jnp.broadcast_to((row - first).astype(F32), (part, count)).astype(BF16)
        tiles.append(jnp.where(place == wanted, ones, zeros))
    return tiles[0] if len(tiles) == 1 else jnp.concatenate(tiles, axis=0)


def regrouped(arrays, lane_bits):
    arrays = [arrays[-j % 16] for j in range(16)]
    for b in range(4):
        arrays = [
            jnp.where(lane_bits[b], arrays[(j - (1 << b)) % 16], arrays[j]) for j in range(16)
        ]
    return arrays


def level_kernel(*refs, pieces, scale):
    place_ref, order_ref = refs[:2]
    blocks = refs[2 : 2 + 2 * pieces]
    src_ref, dst_ref, ops_ref, out_ref, picked_ref, group_ref, sums_ref = refs[2 + 2 * pieces :]
    height, cells = ops_ref.shape[0] // 32, blocks[0].shape[2]
    core, me = place_ref[0], place_ref[1]

    first = 0
    for own_ref, other_ref in zip(blocks[0::2], blocks[1::2]):

        def pick(i, carry, own_ref=own_ref, other_ref=other_ref, first=first):
            z = order_ref[first + i]
            for block_ref, side in ((own_ref, core), (other_ref, 1 - core)):
                h = z * 2 + side
                block = block_ref[i]
                held = block.shape[0]
                for part in range(4):
                    row = src_ref[pl.ds(h, 1), part * 256 : (part + 1) * 256]
                    picked = jnp.dot(block, one_hot(row, cells), preferred_element_type=F32)
                    picked = picked.astype(BF16)
                    picked_ref[h, 2 * part, 0:held] = picked[:, 0:128]
                    picked_ref[h, 2 * part + 1, 0:held] = picked[:, 128:256]
            return carry

        lax.fori_loop(0, own_ref.shape[0], pick, 0)
        first += own_ref.shape[0]

    lane = lax.broadcasted_iota(jnp.int32, (16, 128), 1) // 8
    lane_bits = [(lane >> b) & 1 == 1 for b in range(4)]
    padded = group_ref.shape[1]
    by_column = cells > 256
    place = lax.broadcasted_iota(jnp.int32, (256, cells), 1)

    def add_up(q, carry):
        for half in range(2):
            for top in range(0, padded, 16):
                rows = slice(top, top + 16)
                arrays = [picked_ref[half * 16 + j, q, rows, :] for j in range(16)]
                for j, array in enumerate(regrouped(arrays, lane_bits)):
                    group_ref[j, rows, half * 128 : (half + 1) * 128] = array
        for half in range(2):
            lists = dst_ref[pl.ds(pl.multiple_of(q * 16 + half * 8, 8), 8), :]
            columns = lists.T if by_column else None
            for target in range(2):
                for couple in range(2):
                    sums = []
                    for j in (target * 4 + couple * 2, target * 4 + couple * 2 + 1):
                        terms = group_ref[half * 8 + j, 0:height]
                        if by_column:
                            hot = (place == columns[:, j : j + 1]).astype(BF16)
                            one = jnp.dot(terms, hot, preferred_element_type=F32)
                        else:
                            hot = one_hot(lists[j : j + 1, :], cells)
                            one = lax.dot_general(
                                terms, hot, (((1,), (1,)), ((), ())), preferred_element_type=F32
                            )
                        sums.append(one)
                    distance = (me + 4 - q % 4) % 4
                    start = (distance * 2 + q // 4) * 2 + couple
                    start = pl.multiple_of(start * (2 * height), 2 * height)
                    sums_ref[half * 2 + target, pl.ds(start, 2 * height), :] = jnp.concatenate(
                        sums, axis=0
                    ).astype(BF16)
        return carry

    lax.fori_loop(0, 8, add_up, 0)
    operators = ops_ref[...].T
    for target in range(4):
        total = jnp.dot(operators, sums_ref[target], preferred_element_type=F32)
        out_ref[target] = (total * scale).astype(BF16)


def own_rows(moments):
    height = moments.shape[0] // 4
    return lax.dynamic_slice_in_dim(moments, lax.axis_index("comp") * height, height, 0)


def other_core(array):
    return lax.ppermute(array, "core", [(0, 1), (1, 0)])


def spread_to(block, axis):
    copies = jnp.broadcast_to(block[None], (4,) + block.shape)
    return lax.all_to_all(copies, axis, 0, 0, tiled=True)


def copies_for_z(block):
    return jnp.broadcast_to(block[None], (16,) + block.shape)


def level_partial(pieces, order, src, dst, operators, scale):
    blocks = [block for own, other in pieces for block in (own, other)]
    cells = blocks[0].shape[2]
    width = operators.shape[1]
    height = width // 4
    padded = -(-height // 16) * 16
    smem = pl.BlockSpec(memory_space=pltpu.SMEM)
    vmem = pl.BlockSpec(memory_space=pltpu.VMEM)
    return pl.pallas_call(
        functools.partial(level_kernel, pieces=len(pieces), scale=scale),
        in_specs=[smem, smem] + [vmem] * (len(blocks) + 3),
        out_specs=vmem,
        out_shape=jax.ShapeDtypeStruct((4, width, cells), BF16),
        scratch_shapes=[
            pltpu.VMEM((32, 8, padded, 128), BF16),
            pltpu.VMEM((16, padded, 256), BF16),
            pltpu.VMEM((4, 32 * height, cells), BF16),
        ],
        compiler_params=pltpu.CompilerParams(vmem_limit_bytes=48 * 1024 * 1024),
        cost_estimate=pl.CostEstimate(
            flops=5 * 10**7 * cells, bytes_accessed=6 * 10**6, transcendentals=0
        ),
        name="level",
    )(jnp.stack([lax.axis_index("core"), lax.axis_index("comp")]), order, *blocks, src, dst, operators)


def parts_to_owners(partial):
    groups, width, cells = partial.shape
    pieces = partial.reshape(groups * 4, width // 4, cells)
    return lax.all_to_all(pieces, ("x", "comp"), 0, 0, tiled=True)


def turned(rows):
    return pltpu.roll(rows, 0, 1, stride=8, stride_axis=0)


def crossed(rows, lane_bits):
    rows = jnp.concatenate([rows[0:1]] + [rows[j : j + 1] for j in range(15, 0, -1)], axis=0)
    for b in range(4):
        rows = jnp.where(lane_bits[b], pltpu.roll(rows, 1 << b, 0), rows)
    return rows


def lists_kernel(x_ref, near_ref, far_ref, *out_refs):
    lane = lax.broadcasted_iota(jnp.int32, (16, 128), 1) // 8
    lane_bits = [(lane >> b) & 1 == 1 for b in range(4)]

    def cells_of(codes):
        return codes.astype(F32).astype(jnp.int32) + CODE_OFFSET

    for part in range(4):
        for half in range(2):
            near_lists = [cells_of(near_ref[part, (x_ref[0] + 4 - g) % 4, half]) for g in range(4)]
            for level in range(2):
                src_ref, dst_ref = out_refs[2 * level : 2 * level + 2]
                lanes = slice(half * 128, (half + 1) * 128)
                hs = slice(half * 16, (half + 1) * 16)

                def near(value):
                    kind = (level * 2 + value) * 4
                    return jnp.concatenate(
                        [lists[kind : kind + 4] for lists in near_lists], axis=0
                    )

                def far(value):
                    return cells_of(far_ref[part, level * 2 + value, hs, :])

                src_ref[hs, part * 128 : (part + 1) * 128] = crossed(
                    turned(near(0)), lane_bits
                )
                dst_ref[part * 16 : (part + 1) * 16, lanes] = turned(near(1))
                src_ref[hs, (part + 4) * 128 : (part + 5) * 128] = turned(far(0))
                dst_ref[(part + 4) * 16 : (part + 5) * 16, lanes] = crossed(
                    turned(far(1)), lane_bits
                )


def slot_messages(fine_pairs, coarse_pairs):
    both = jnp.stack([fine_pairs, coarse_pairs])
    first, second, alive = both[:, 0], both[:, 1], both[:, 2] == 1
    classes = first.shape[1]

    def slots(source, target):
        lists = jnp.stack([jnp.where(alive, source - CODE_OFFSET, NO_CELL), target - CODE_OFFSET], 1)
        lists = lists.astype(BF16).reshape(2, 2, classes, 4, 32, CAP)
        return jnp.pad(lists, [(0, 0)] * 5 + [(0, 8 - CAP)], constant_values=NO_CELL)

    near = slots(second, first).reshape(2, 2, classes, 4, 2, 128)
    near = near.transpose(3, 4, 0, 1, 2, 5).reshape(4, 8 * classes, 128)
    far = slots(first, second).transpose(4, 0, 1, 3, 2, 5).reshape(4, 4, 8, 128)
    far = jnp.concatenate([far[:, j] for j in range(4)], axis=-1)
    return near, far


def passed(array, axis, distance):
    if distance == 0:
        return array
    count = lax.axis_size(axis)
    return lax.ppermute(array, axis, [(i, (i + distance) % count) for i in range(count)])


def parts_for(array, name, axis):
    me = lax.axis_index(name)
    return [
        lax.dynamic_index_in_dim(array, (me + distance) % 4, axis, keepdims=False)
        for distance in range(4)
    ]


def exchanged(parts, name, distances):
    return jnp.stack(
        [
            passed(part, name, distance) if distance in distances else part
            for distance, part in enumerate(parts)
        ]
    )


def lists_from_chip_and_comp(near, blocks):
    rows = blocks[:, 72:].reshape(4, 4, 2, 4, -1)
    rows = lax.dynamic_slice_in_dim(rows, lax.axis_index("zl") * 128, 128, 4)
    rows = rows.transpose(2, 0, 1, 3, 4).reshape(2, 64, 128)
    near = jnp.broadcast_to(near.reshape(1, 128, 128), (2, 128, 128))
    rows = jnp.concatenate([rows, near], axis=1)
    rows = jnp.broadcast_to(rows[:, None], (2, 4, 192, 128)).reshape(8, 192, 128)
    rows = lax.all_to_all(rows, ("core", "comp"), 0, 0, tiled=True).reshape(2, 4, 192, 128)
    near = lax.dynamic_index_in_dim(rows[:, :, 64:], lax.axis_index("core"), 0, keepdims=False)
    far = rows[:, :, :64].reshape(2, 4, 4, 4, 4, 128).transpose(1, 4, 3, 2, 0, 5)
    return near.reshape(4, 4, 2, 16, 128), far.reshape(4, 4, 32, 128)


def slot_lists(near, far):
    vmem = pl.BlockSpec(memory_space=pltpu.VMEM)
    return pl.pallas_call(
        lists_kernel,
        in_specs=[pl.BlockSpec(memory_space=pltpu.SMEM), vmem, vmem],
        out_specs=[vmem] * 4,
        out_shape=[
            jax.ShapeDtypeStruct((32, 1024), jnp.int32),
            jax.ShapeDtypeStruct((128, 256), jnp.int32),
        ]
        * 2,
        name="lists",
    )(lax.axis_index("x").reshape(1), near, far)


def operator_parts(translations):
    classes, width, _ = translations.shape
    both = jnp.stack([translations, translations.swapaxes(1, 2)])
    return parts_for(both.reshape(2, classes, 4, width // 4, width), "comp", 2)


def per_device(fine_moments, translations, shifts_up, fine_pairs, coarse_pairs, child_links):
    near, far = slot_messages(fine_pairs, coarse_pairs)
    rows = own_rows(fine_moments)
    copies = jnp.broadcast_to(rows[None], (4,) + rows.shape)
    four = lax.all_to_all(jnp.concatenate([copies, far], axis=1), "zh", 0, 0, tiled=True)
    slot, edge = edge_from_before(fine_moments, child_links)
    near, operators = parts_for(near, "x", 0), operator_parts(translations)
    near[1] = passed(near[1], "x", 1)
    operators[2] = passed(operators[2], "comp", 2)
    four, near, operators = lax.optimization_barrier((four, near, operators))
    fine = spread_to(four, "zl").reshape((16,) + four.shape[1:])
    near = exchanged(near, "x", (2, 3))
    operators = exchanged(operators, "comp", (1, 3)).reshape(-1, fine_moments.shape[0])
    coarse_moments = upward(fine_moments, slot, edge, shifts_up)
    near, operators, fine = lax.optimization_barrier((near, operators, fine))
    fine_other = other_core(fine)
    fine_src, fine_dst, coarse_src, coarse_dst = slot_lists(*lists_from_chip_and_comp(near, fine))
    coarse = copies_for_z(own_rows(coarse_moments))
    coarse, fine_src = lax.optimization_barrier((coarse, fine_src))
    place = jnp.arange(16, dtype=jnp.int32)
    order = place % 4 * 4 + place // 4
    fine_partial = level_partial([(fine, fine_other)], order, fine_src, fine_dst, operators, 1.0)

    coarse = lax.all_to_all(coarse, ("zh", "zl"), 0, 0, tiled=True)
    coarse, fine_partial = lax.optimization_barrier((coarse, fine_partial))
    other = other_core(coarse)
    coarse_partial = level_partial(
        [(coarse, other)], place, coarse_src, coarse_dst, operators, 0.5
    )
    fine_parts = parts_to_owners(fine_partial)
    coarse_partial, fine_parts = lax.optimization_barrier((coarse_partial, fine_parts))
    coarse_parts = parts_to_owners(coarse_partial)
    fine_locals = jnp.sum(fine_parts.astype(F32), axis=0)
    coarse_locals = jnp.sum(coarse_parts.astype(F32), axis=0)
    return (fine_locals, coarse_moments, coarse_locals)


def solution(mesh):
    split = Mesh(mesh.devices.reshape(4, 4, 4, 2, 4), CELLS + ("comp",))
    return jax.shard_map(
        per_device,
        mesh=split,
        in_specs=(
            P(None, CELLS),
            P("comp", None, None),
            P(),
            P(None, "comp", CELLS),
            P(None, "comp", CELLS),
            P(None, CELLS),
        ),
        out_specs=(P("comp", CELLS), P(None, CELLS), P("comp", CELLS)),
        check_vma=False,
    )
```

```python
import functools

import jax
import jax.numpy as jnp
from jax import lax
from jax.experimental import pallas as pl
from jax.experimental.pallas import tpu as pltpu
from jax.sharding import Mesh
from jax.sharding import PartitionSpec as P

CAP = 6
CODE_OFFSET = 256
NO_CELL = 1024
CELLS = ("x", "zh", "zl", "core")
BF16 = jnp.bfloat16
F32 = jnp.float32


def upward_kernel(moments_ref, slot_ref, shifts_ref, out_ref):
    octants, width, _ = shifts_ref.shape
    coarse = out_ref.shape[1]
    spots = octants * coarse
    rows = lax.broadcasted_iota(jnp.int32, (spots, slot_ref.shape[1]), 0)
    hot = (rows == slot_ref[0:1, :]).astype(BF16)
    placed = lax.dot_general(
        moments_ref[...], hot, (((1,), (1,)), ((), ())), preferred_element_type=F32
    ).astype(BF16)
    total = jnp.zeros((width, coarse), F32)
    for octant in range(octants):
        part = placed[:, octant * coarse : (octant + 1) * coarse]
        total = total + jnp.dot(shifts_ref[octant], part, preferred_element_type=F32)
    out_ref[...] = total.astype(BF16)


def edge_from_before(moments, child_links):
    coarse = moments.shape[1] // 4
    group = lax.axis_index(CELLS)
    devices = lax.axis_size(CELLS)
    parent = child_links[0] - group * coarse
    octant = child_links[1]
    inside = parent < coarse
    slot = jnp.where(inside, octant * coarse + parent, -1)
    code = jnp.where(inside, -1, octant)[-4:].astype(F32)
    edge = jnp.concatenate([moments[:, -4:].T.astype(F32), code[:, None]], axis=1)
    return slot, lax.ppermute(edge, CELLS, [(i, i + 1) for i in range(devices - 1)])


def upward(moments, slot, edge, shifts_up):
    width, fine = moments.shape
    coarse = fine // 4
    edge_code = edge[:, width].astype(jnp.int32)
    edge_slot = jnp.where(edge_code >= 0, edge_code * coarse, -1)
    edge_moments = edge[:, :width].T.astype(BF16)
    pad = 124
    slots = jnp.concatenate([slot, edge_slot, jnp.full((pad,), -1, jnp.int32)])
    extended = jnp.concatenate([moments, edge_moments, jnp.zeros((width, pad), BF16)], axis=1)
    return pl.pallas_call(
        upward_kernel,
        out_shape=jax.ShapeDtypeStruct((width, coarse), BF16),
        compiler_params=pltpu.CompilerParams(vmem_limit_bytes=48 * 1024 * 1024),
        cost_estimate=pl.CostEstimate(flops=8 * 10**8, bytes_accessed=2 * 10**6, transcendentals=0),
        name="upward",
    )(extended, slots.reshape(1, -1), shifts_up)


def one_hot(row, cells):
    count = row.shape[1]
    part = min(cells, 256)
    place = lax.broadcasted_iota(jnp.int32, (part, count), 0).astype(F32).astype(BF16)
    ones, zeros = jnp.ones((part, count), BF16), jnp.zeros((part, count), BF16)
    tiles = []
    for first in range(0, cells, part):
        wanted = jnp.broadcast_to((row - first).astype(F32), (part, count)).astype(BF16)
        tiles.append(jnp.where(place == wanted, ones, zeros))
    return tiles[0] if len(tiles) == 1 else jnp.concatenate(tiles, axis=0)


def regrouped(arrays, lane_bits):
    arrays = [arrays[-j % 16] for j in range(16)]
    for b in range(4):
        arrays = [
            jnp.where(lane_bits[b], arrays[(j - (1 << b)) % 16], arrays[j]) for j in range(16)
        ]
    return arrays


def level_kernel(*refs, pieces, scale):
    place_ref, order_ref = refs[:2]
    blocks = refs[2 : 2 + 2 * pieces]
    src_ref, dst_ref, ops_ref, out_ref, picked_ref, group_ref, sums_ref = refs[2 + 2 * pieces :]
    height, cells = ops_ref.shape[0] // 32, blocks[0].shape[2]
    core, me = place_ref[0], place_ref[1]

    first = 0
    for own_ref, other_ref in zip(blocks[0::2], blocks[1::2]):

        def pick(i, carry, own_ref=own_ref, other_ref=other_ref, first=first):
            z = order_ref[first + i]
            for block_ref, side in ((own_ref, core), (other_ref, 1 - core)):
                h = z * 2 + side
                block = block_ref[i]
                held = block.shape[0]
                for part in range(4):
                    row = src_ref[pl.ds(h, 1), part * 256 : (part + 1) * 256]
                    picked = jnp.dot(block, one_hot(row, cells), preferred_element_type=F32)
                    picked = picked.astype(BF16)
                    picked_ref[h, 2 * part, 0:held] = picked[:, 0:128]
                    picked_ref[h, 2 * part + 1, 0:held] = picked[:, 128:256]
            return carry

        lax.fori_loop(0, own_ref.shape[0], pick, 0)
        first += own_ref.shape[0]

    lane = lax.broadcasted_iota(jnp.int32, (16, 128), 1) // 8
    lane_bits = [(lane >> b) & 1 == 1 for b in range(4)]
    padded = group_ref.shape[1]
    by_column = cells > 256
    place = lax.broadcasted_iota(jnp.int32, (256, cells), 1)

    def add_up(q, carry):
        for half in range(2):
            for top in range(0, padded, 16):
                rows = slice(top, top + 16)
                arrays = [picked_ref[half * 16 + j, q, rows, :] for j in range(16)]
                for j, array in enumerate(regrouped(arrays, lane_bits)):
                    group_ref[j, rows, half * 128 : (half + 1) * 128] = array
        for half in range(2):
            lists = dst_ref[pl.ds(pl.multiple_of(q * 16 + half * 8, 8), 8), :]
            columns = lists.T if by_column else None
            for target in range(2):
                for couple in range(2):
                    sums = []
                    for j in (target * 4 + couple * 2, target * 4 + couple * 2 + 1):
                        terms = group_ref[half * 8 + j, 0:height]
                        if by_column:
                            hot = (place == columns[:, j : j + 1]).astype(BF16)
                            one = jnp.dot(terms, hot, preferred_element_type=F32)
                        else:
                            hot = one_hot(lists[j : j + 1, :], cells)
                            one = lax.dot_general(
                                terms, hot, (((1,), (1,)), ((), ())), preferred_element_type=F32
                            )
                        sums.append(one)
                    distance = (me + 4 - q % 4) % 4
                    start = (distance * 2 + q // 4) * 2 + couple
                    start = pl.multiple_of(start * (2 * height), 2 * height)
                    sums_ref[half * 2 + target, pl.ds(start, 2 * height), :] = jnp.concatenate(
                        sums, axis=0
                    ).astype(BF16)
        return carry

    lax.fori_loop(0, 8, add_up, 0)
    operators = ops_ref[...].T
    for target in range(4):
        total = jnp.dot(operators, sums_ref[target], preferred_element_type=F32)
        out_ref[target] = (total * scale).astype(BF16)


def own_rows(moments):
    height = moments.shape[0] // 4
    return lax.dynamic_slice_in_dim(moments, lax.axis_index("comp") * height, height, 0)


def other_core(array):
    return lax.ppermute(array, "core", [(0, 1), (1, 0)])


def spread_to(block, axis):
    copies = jnp.broadcast_to(block[None], (4,) + block.shape)
    return lax.all_to_all(copies, axis, 0, 0, tiled=True)


def copies_for_z(block):
    return jnp.broadcast_to(block[None], (16,) + block.shape)


def level_partial(pieces, order, src, dst, operators, scale):
    blocks = [block for own, other in pieces for block in (own, other)]
    cells = blocks[0].shape[2]
    width = operators.shape[1]
    height = width // 4
    padded = -(-height // 16) * 16
    smem = pl.BlockSpec(memory_space=pltpu.SMEM)
    vmem = pl.BlockSpec(memory_space=pltpu.VMEM)
    return pl.pallas_call(
        functools.partial(level_kernel, pieces=len(pieces), scale=scale),
        in_specs=[smem, smem] + [vmem] * (len(blocks) + 3),
        out_specs=vmem,
        out_shape=jax.ShapeDtypeStruct((4, width, cells), BF16),
        scratch_shapes=[
            pltpu.VMEM((32, 8, padded, 128), BF16),
            pltpu.VMEM((16, padded, 256), BF16),
            pltpu.VMEM((4, 32 * height, cells), BF16),
        ],
        compiler_params=pltpu.CompilerParams(vmem_limit_bytes=48 * 1024 * 1024),
        cost_estimate=pl.CostEstimate(
            flops=5 * 10**7 * cells, bytes_accessed=6 * 10**6, transcendentals=0
        ),
        name="level",
    )(jnp.stack([lax.axis_index("core"), lax.axis_index("comp")]), order, *blocks, src, dst, operators)


def parts_to_owners(partial):
    groups, width, cells = partial.shape
    pieces = partial.reshape(groups * 4, width // 4, cells)
    return lax.all_to_all(pieces, ("x", "comp"), 0, 0, tiled=True)


def turned(rows):
    return pltpu.roll(rows, 0, 1, stride=8, stride_axis=0)


def crossed(rows, lane_bits):
    rows = jnp.concatenate([rows[0:1]] + [rows[j : j + 1] for j in range(15, 0, -1)], axis=0)
    for b in range(4):
        rows = jnp.where(lane_bits[b], pltpu.roll(rows, 1 << b, 0), rows)
    return rows


def lists_kernel(place_ref, near_ref, far_ref, *out_refs):
    lane = lax.broadcasted_iota(jnp.int32, (16, 128), 1) // 8
    lane_bits = [(lane >> b) & 1 == 1 for b in range(4)]

    def cells_of(codes):
        return codes.astype(F32).astype(jnp.int32) + CODE_OFFSET

    for part in range(4):
        for half in range(2):
            near_lists = []
            for g in range(4):
                first = 64 + ((place_ref[0] + 4 - g) % 4 * 2 + half) * 16
                rows = pl.ds(pl.multiple_of(first, 16), 16)
                near_lists.append(cells_of(near_ref[place_ref[1], part, rows, :]))
            for level in range(2):
                src_ref, dst_ref = out_refs[2 * level : 2 * level + 2]
                lanes = slice(half * 128, (half + 1) * 128)
                hs = slice(half * 16, (half + 1) * 16)

                def near(value):
                    kind = (level * 2 + value) * 4
                    return jnp.concatenate(
                        [lists[kind : kind + 4] for lists in near_lists], axis=0
                    )

                def far(value):
                    return cells_of(far_ref[part, level * 2 + value, hs, :])

                src_ref[hs, part * 128 : (part + 1) * 128] = crossed(
                    turned(near(0)), lane_bits
                )
                dst_ref[part * 16 : (part + 1) * 16, lanes] = turned(near(1))
                src_ref[hs, (part + 4) * 128 : (part + 5) * 128] = turned(far(0))
                dst_ref[(part + 4) * 16 : (part + 5) * 16, lanes] = crossed(
                    turned(far(1)), lane_bits
                )


def slot_messages(fine_pairs, coarse_pairs):
    both = jnp.stack([fine_pairs, coarse_pairs])
    first, second, alive = both[:, 0], both[:, 1], both[:, 2] == 1
    classes = first.shape[1]

    def slots(source, target):
        lists = jnp.stack([jnp.where(alive, source - CODE_OFFSET, NO_CELL), target - CODE_OFFSET], 1)
        lists = lists.astype(BF16).reshape(2, 2, classes, 4, 32, CAP)
        return jnp.pad(lists, [(0, 0)] * 5 + [(0, 8 - CAP)], constant_values=NO_CELL)

    near = slots(second, first).reshape(2, 2, classes, 4, 2, 128)
    near = near.transpose(3, 4, 0, 1, 2, 5).reshape(4, 8 * classes, 128)
    far = slots(first, second).transpose(4, 0, 1, 3, 2, 5).reshape(4, 4, 8, 128)
    far = jnp.concatenate([far[:, j] for j in range(4)], axis=-1)
    return near, far


def passed(array, axis, distance):
    if distance == 0:
        return array
    count = lax.axis_size(axis)
    return lax.ppermute(array, axis, [(i, (i + distance) % count) for i in range(count)])


def parts_for(array, name, axis):
    me = lax.axis_index(name)
    return [
        lax.dynamic_index_in_dim(array, (me + distance) % 4, axis, keepdims=False)
        for distance in range(4)
    ]


def exchanged(parts, name, distances):
    return jnp.stack(
        [
            passed(part, name, distance) if distance in distances else part
            for distance, part in enumerate(parts)
        ]
    )


def lists_message(near, blocks):
    rows = blocks[:, 72:].reshape(4, 4, 2, 4, -1)
    rows = lax.dynamic_slice_in_dim(rows, lax.axis_index("zl") * 128, 128, 4)
    rows = rows.transpose(2, 0, 1, 3, 4).reshape(2, 64, 128)
    near = jnp.broadcast_to(near.reshape(1, 128, 128), (2, 128, 128))
    rows = jnp.concatenate([rows, near], axis=1)
    return jnp.broadcast_to(rows[:, None], (2, 4, 192, 128)).reshape(8, 192, 128)


def lists_from_chip_and_comp(message):
    rows = lax.all_to_all(message, ("core", "comp"), 0, 0, tiled=True).reshape(2, 4, 192, 128)
    far = rows[:, :, :64].reshape(2, 4, 4, 4, 4, 128).transpose(1, 4, 3, 2, 0, 5)
    return rows, far.reshape(4, 4, 32, 128)


def slot_lists(near, far):
    vmem = pl.BlockSpec(memory_space=pltpu.VMEM)
    return pl.pallas_call(
        lists_kernel,
        in_specs=[pl.BlockSpec(memory_space=pltpu.SMEM), vmem, vmem],
        out_specs=[vmem] * 4,
        out_shape=[
            jax.ShapeDtypeStruct((32, 1024), jnp.int32),
            jax.ShapeDtypeStruct((128, 256), jnp.int32),
        ]
        * 2,
        name="lists",
    )(jnp.stack([lax.axis_index("x"), lax.axis_index("core")]), near, far)


def operator_parts(translations):
    classes, width, _ = translations.shape
    both = jnp.stack([translations, translations.swapaxes(1, 2)])
    return parts_for(both.reshape(2, classes, 4, width // 4, width), "comp", 2)


def per_device(fine_moments, translations, shifts_up, fine_pairs, coarse_pairs, child_links):
    near, far = slot_messages(fine_pairs, coarse_pairs)
    rows = own_rows(fine_moments)
    copies = jnp.broadcast_to(rows[None], (4,) + rows.shape)
    four = lax.all_to_all(jnp.concatenate([copies, far], axis=1), "zh", 0, 0, tiled=True)
    slot, edge = edge_from_before(fine_moments, child_links)
    near, operators = parts_for(near, "x", 0), operator_parts(translations)
    near[1] = passed(near[1], "x", 1)
    operators[2] = passed(operators[2], "comp", 2)
    four, near, operators = lax.optimization_barrier((four, near, operators))
    fine = spread_to(four, "zl").reshape((16,) + four.shape[1:])
    near = exchanged(near, "x", (2, 3))
    operators = exchanged(operators, "comp", (1, 3)).reshape(-1, fine_moments.shape[0])
    coarse_moments = upward(fine_moments, slot, edge, shifts_up)
    near, operators, fine = lax.optimization_barrier((near, operators, fine))
    message, fine = lax.optimization_barrier((lists_message(near, fine), fine))
    fine_other = other_core(fine)
    lists = slot_lists(*lists_from_chip_and_comp(message))
    fine_src, fine_dst, coarse_src, coarse_dst = lists
    coarse = copies_for_z(own_rows(coarse_moments))
    coarse, fine_src = lax.optimization_barrier((coarse, fine_src))
    place = jnp.arange(16, dtype=jnp.int32)
    order = place % 4 * 4 + place // 4
    fine_partial = level_partial([(fine, fine_other)], order, fine_src, fine_dst, operators, 1.0)

    coarse = lax.all_to_all(coarse, ("zh", "zl"), 0, 0, tiled=True)
    coarse, fine_partial = lax.optimization_barrier((coarse, fine_partial))
    other = other_core(coarse)
    coarse_partial = level_partial(
        [(coarse, other)], place, coarse_src, coarse_dst, operators, 0.5
    )
    fine_parts = parts_to_owners(fine_partial)
    coarse_partial, fine_parts = lax.optimization_barrier((coarse_partial, fine_parts))
    coarse_parts = parts_to_owners(coarse_partial)
    fine_locals = jnp.sum(fine_parts.astype(F32), axis=0)
    coarse_locals = jnp.sum(coarse_parts.astype(F32), axis=0)
    return (fine_locals, coarse_moments, coarse_locals)


def solution(mesh):
    split = Mesh(mesh.devices.reshape(4, 4, 4, 2, 4), CELLS + ("comp",))
    return jax.shard_map(
        per_device,
        mesh=split,
        in_specs=(
            P(None, CELLS),
            P("comp", None, None),
            P(),
            P(None, "comp", CELLS),
            P(None, "comp", CELLS),
            P(None, CELLS),
        ),
        out_specs=(P("comp", CELLS), P(None, CELLS), P("comp", CELLS)),
        check_vma=False,
    )
```
